256 devices in a mesh: fsdp: 64 (over z, x, core), rep: 4 (over y).
Axes of the slice: x: 4, y: 4, z: 8, core: 2. Of those that a mesh axis runs over, the one named last changes fastest.
Arguments:
- replica_grads: bfloat16 [4, 2048, 18944], P('rep', 'fsdp'), may hold values from -2 to 2
- block_owner: int32 [4, 37], replicated, may hold values from 0 to 63, as said below
- left_factor: float32 [64, 4, 1, 512, 512], P('fsdp', 'rep'), may hold values from -1 to 21, as said below
- right_factor: float32 [64, 4, 1, 512, 512], P('fsdp', 'rep'), may hold values from -1 to 21, as said below
- left_root: bfloat16 [64, 4, 1, 512, 512], P('fsdp', 'rep'), may hold values from -1 to 3, as said below
- right_root: bfloat16 [64, 4, 1, 512, 512], P('fsdp', 'rep'), may hold values from -1 to 3, as said below
- moment: float32 [64, 4, 1, 512, 512], P('fsdp', 'rep'), may hold values from 1e-05 to 0.01
Outputs:
- direction: bfloat16 [2048, 18944], P('fsdp')
- left_new: float32 [64, 4, 1, 512, 512], P('fsdp', 'rep')
- right_new: float32 [64, 4, 1, 512, 512], P('fsdp', 'rep')
- moment_new: float32 [64, 4, 1, 512, 512], P('fsdp', 'rep')
The draws below stay inside these ranges and needn't reach their ends.
Inputs may be any that keep to these rules, and one draw needn't show every extreme that they name: `block_owner`: within each of the 4 block rows no owner holds more than 1 of the 37 blocks, and some owner holds exactly 1. `left_factor`: Symmetric. `right_factor`: Symmetric. `left_root`: Symmetric. `right_root`: Symmetric.
All inputs are finite; a program needn't handle non-finite values.
Results may differ from the reference program's by a relative error of at most 0.017.
Values may be sent and summed in bfloat16 or wider, within the bound.
A program may use at most 128 MiB of HBM per device.

```python
import math
import jax
import jax.numpy as jnp
from jax import lax

FF = 18944
B = 512
ROWS = 2048
CB = 37
SPR = 1
N_FSDP = 64
N_REP = 4


def symmetric(noise, diagonal, spread):
    eye_matrix = jnp.eye(noise.shape[-1], dtype=jnp.float32)
    return (noise + jnp.swapaxes(noise, -1, -2)) * spread + diagonal[..., None] * eye_matrix


def draw_replica_grads(key, part):
    key = jax.random.fold_in(key, 1)
    key_own, key_rows, key_cols = jax.random.split(key, 3)
    shape = (N_REP, ROWS, FF)
    row_scale = jnp.exp(jax.random.uniform(key_rows, (ROWS,), jnp.float32, math.log(0.3), math.log(3.0)))
    col_scale = jnp.exp(jax.random.uniform(key_cols, (FF,), jnp.float32, math.log(0.3), math.log(3.0)))
    values = jnp.clip(jax.random.normal(key_own, shape, jnp.float32), -4.0, 4.0)
    return (0.02 * values * row_scale[None, :, None] * col_scale[None, None, :]).astype(jnp.bfloat16)


def draw_block_owner(key, part):
    key = jax.random.fold_in(key, 2)
    row_keys = jax.random.split(key, N_REP)

    def one_row(row_key):
        return (jax.random.permutation(row_key, N_FSDP * SPR)[:CB] // SPR).astype(jnp.int32)
    return jax.vmap(one_row)(row_keys)


def draw_left_factor(key, part):
    key = jax.random.fold_in(key, 3)
    key_noise, key_diag = jax.random.split(key)
    shape = (N_FSDP, N_REP, SPR, B, B)
    noise = jnp.clip(jax.random.normal(key_noise, shape, jnp.float32), -4.0, 4.0)
    diagonal = jnp.exp(jax.random.uniform(key_diag, shape[:-1], jnp.float32, 0.0, math.log(20.0)))
    return symmetric(noise, diagonal, 0.07)


def draw_right_factor(key, part):
    key = jax.random.fold_in(key, 4)
    key_noise, key_diag = jax.random.split(key)
    shape = (N_FSDP, N_REP, SPR, B, B)
    noise = jnp.clip(jax.random.normal(key_noise, shape, jnp.float32), -4.0, 4.0)
    diagonal = jnp.exp(jax.random.uniform(key_diag, shape[:-1], jnp.float32, 0.0, math.log(20.0)))
    return symmetric(noise, diagonal, 0.07)


def draw_left_root(key, part):
    key = jax.random.fold_in(key, 5)
    key_noise, key_diag = jax.random.split(key)
    shape = (N_FSDP, N_REP, SPR, B, B)
    noise = jnp.clip(jax.random.normal(key_noise, shape, jnp.float32), -4.0, 4.0)
    diagonal = jnp.exp(jax.random.uniform(key_diag, shape[:-1], jnp.float32, math.log(0.5), math.log(2.0)))
    return symmetric(noise, diagonal, 0.5 / math.sqrt(2.0 * B)).astype(jnp.bfloat16)


def draw_right_root(key, part):
    key = jax.random.fold_in(key, 6)
    key_noise, key_diag = jax.random.split(key)
    shape = (N_FSDP, N_REP, SPR, B, B)
    noise = jnp.clip(jax.random.normal(key_noise, shape, jnp.float32), -4.0, 4.0)
    diagonal = jnp.exp(jax.random.uniform(key_diag, shape[:-1], jnp.float32, math.log(0.5), math.log(2.0)))
    return symmetric(noise, diagonal, 0.5 / math.sqrt(2.0 * B)).astype(jnp.bfloat16)


def steps_of(key, extent, shards, low, top_value):
    level = 1.0
    for dim, shards_of in shards:
        draws = jax.random.uniform(jax.random.fold_in(jax.random.fold_in(key, 6), dim), (shards_of,), jnp.float32, low / len(shards), top_value / len(shards))
        level = level * jnp.repeat(jnp.exp(draws), extent[dim] // shards_of).reshape((-1,) + (1,) * (len(extent) - 1 - dim))
    return level


def setup_inputs(seed: int = 0) -> dict:
    key_of = jax.random.split(jax.random.key(seed), 8)
    return {
        "replica_grads": draw_replica_grads(jax.random.fold_in(key_of[7], 71), 0),
        "block_owner": draw_block_owner(jax.random.fold_in(key_of[7], 71), 0),
        "left_factor": draw_left_factor(jax.random.fold_in(key_of[7], 71), 0),
        "right_factor": draw_right_factor(jax.random.fold_in(key_of[7], 71), 0),
        "left_root": draw_left_root(jax.random.fold_in(key_of[7], 71), 0),
        "right_root": draw_right_root(jax.random.fold_in(key_of[7], 71), 0),
        "moment": jnp.clip(jnp.exp(math.log(0.01) - 6.9077553 * jax.random.uniform(key_of[6], (N_FSDP, N_REP, SPR, B, B), jnp.float32) ** steps_of(key_of[6], (N_FSDP, N_REP, SPR, B, B), ((0, 64), (1, 4)), -0.2, 0.2)), 9.999999747378752e-06, 0.01),
    }


stat_decay = 0.9
graft_decay = 0.99
adam_epsilon = 1e-08
graft_epsilon = 1e-06

def slot_ranks(block_owner):
    columns = jnp.arange(block_owner.shape[1], dtype=jnp.int32)
    earlier = (block_owner[:, :, None] == block_owner[:, None, :]) & (columns[None, None, :] < columns[None, :, None])
    return lax.optimization_barrier(jnp.sum(earlier.astype(jnp.int32), axis=2)).astype(jnp.int32)

def update_block(gradient, left_old, right_old, left_root, right_root, moment_old):
    highest = lax.Precision.HIGHEST
    left_new = stat_decay * left_old + (1.0 - stat_decay) * jnp.dot(gradient, gradient.T, precision=highest)
    right_new = stat_decay * right_old + (1.0 - stat_decay) * jnp.dot(gradient.T, gradient, precision=highest)
    moment_new = graft_decay * moment_old + (1.0 - graft_decay) * gradient * gradient
    adam_step = gradient / (jnp.sqrt(moment_new) + adam_epsilon)
    low_grad = gradient.astype(jnp.bfloat16)
    half_done = jnp.dot(left_root, low_grad, preferred_element_type=jnp.float32).astype(jnp.bfloat16)
    conditioned = jnp.dot(half_done, right_root, preferred_element_type=jnp.float32)
    graft_scale = jnp.sqrt((jnp.mean(adam_step * adam_step) + graft_epsilon) / (jnp.mean(conditioned * conditioned) + graft_epsilon))
    return (left_new, right_new, moment_new, (graft_scale * conditioned).astype(jnp.bfloat16))

def reference(replica_grads, block_owner, left_factor, right_factor, left_root, right_root, moment):
    summed_grad = lax.optimization_barrier(jnp.sum(replica_grads.astype(jnp.float32), axis=0))
    slot_rank = slot_ranks(block_owner)
    columns = jnp.arange(CB, dtype=jnp.int32)
    slot_grid = jnp.arange(N_FSDP * N_REP * SPR, dtype=jnp.int32)

    def one_slot(position):
        holder = position // (N_REP * SPR)
        block_row = position // SPR % N_REP
        slot_pos = position % SPR
        row_owner = block_owner[block_row]
        row_slot = slot_rank[block_row]
        matches = (row_owner == holder) & (row_slot == slot_pos)
        present = jnp.sum(matches.astype(jnp.float32))
        column = jnp.sum(jnp.where(matches, columns, 0)).astype(jnp.int32)
        gradient = lax.dynamic_slice(summed_grad, ((block_row * B).astype(jnp.int32), (column * B).astype(jnp.int32)), (B, B)) * present
        return update_block(gradient, left_factor[holder, block_row, slot_pos], right_factor[holder, block_row, slot_pos], left_root[holder, block_row, slot_pos], right_root[holder, block_row, slot_pos], moment[holder, block_row, slot_pos])
    left_new, right_new, moment_new, step_blocks = lax.map(one_slot, slot_grid)
    state_shape = (N_FSDP, N_REP, SPR, B, B)
    flat_index = ((block_owner * N_REP + jnp.arange(N_REP, dtype=jnp.int32)[:, None]) * SPR + slot_rank).astype(jnp.int32)
    blocks = step_blocks[flat_index]
    direction = blocks.transpose(0, 2, 1, 3).reshape(ROWS, FF)
    return (direction, left_new.reshape(state_shape), right_new.reshape(state_shape), moment_new.reshape(state_shape))
```

```python
import functools

import jax
import jax.numpy as jnp
from jax import lax
from jax.experimental import pallas as pl
from jax.experimental.pallas import tpu as pltpu
from jax.sharding import PartitionSpec as P

MESH = pl.DeviceIdType.MESH

stat_decay = 0.9
graft_decay = 0.99
adam_epsilon = 1e-08
graft_epsilon = 1e-06

bf16 = jnp.bfloat16
f32 = jnp.float32


def remote(src, dst, send_sem, recv_sem, where):
    return pltpu.make_async_remote_copy(
        src_ref=src,
        dst_ref=dst,
        send_sem=send_sem,
        recv_sem=recv_sem,
        device_id=where,
        device_id_type=MESH,
    )


def kernel(
    sizes,
    pick_ref,
    owner_ref,
    grads_hbm,
    left_root_hbm,
    right_root_hbm,
    moment_hbm,
    direction_ref,
    g_out_ref,
    grads,
    left_root,
    right_root,
    moment,
    stage,
    mine,
    parts,
    outbox,
    g_land,
    conditioned,
    stepped,
    relay,
    arrived,
    chosen,
    load_sem,
    part_send,
    part_recv,
    out_send,
    out_recv,
    relay_send,
    relay_recv,
    back_send,
    back_recv,
    choice_send,
    choice_recv,
    g_sem,
):
    owners, reps, cols, rows, block, lane, per_row = sizes
    f = lax.axis_index("fsdp")
    y = lax.axis_index("rep")
    home = f // per_row
    place = f % per_row

    loads = [
        pltpu.make_async_copy(grads_hbm, grads, load_sem.at[0]),
        pltpu.make_async_copy(left_root_hbm, left_root, load_sem.at[1]),
        pltpu.make_async_copy(right_root_hbm, right_root, load_sem.at[2]),
        pltpu.make_async_copy(moment_hbm, moment, load_sem.at[3]),
    ]
    for load in loads:
        load.start()

    barrier = pltpu.get_barrier_semaphore()

    def greet(to_f, to_y):
        pl.semaphore_signal(barrier, inc=1, device_id=(to_f, to_y), device_id_type=MESH)

    @pl.loop(1, owners)
    def _(k):
        greet((f + k) % owners, y)

    for d in range(1, reps):
        other = (y + d) % reps

        @pl.loop(0, per_row)
        def _(i):
            greet(per_row * y + i, other)

        @pl.when(home != y)
        def _():
            greet(f, other)

    loads[0].wait()
    for d in range(1, reps):
        peer = (y + d) % reps

        @pl.loop(0, cols)
        def _(c):
            start = pl.multiple_of(c * block + peer * lane, lane)
            stage[d - 1, c] = grads[:, pl.ds(start, lane)]

    @pl.loop(0, cols)
    def _(c):
        start = pl.multiple_of(c * block + y * lane, lane)
        mine[c] = grads[:, pl.ds(start, lane)]

    nothing = jnp.zeros((rows, lane), bf16)
    mine[cols] = nothing
    for d in range(reps - 1):
        parts[d, cols] = nothing

    own_plane = home == y
    plane_and_replicas = owners - 1 + reps - 1
    pl.semaphore_wait(
        barrier, jnp.where(own_plane, plane_and_replicas, plane_and_replicas + owners - 1)
    )

    for d in range(1, reps):
        remote(
            stage.at[d - 1],
            parts.at[d - 1, pl.ds(0, cols)],
            part_send.at[d - 1],
            part_recv.at[d - 1],
            (f, (y + d) % reps),
        ).start()

    for d in range(1, reps):
        remote(
            stage.at[d - 1],
            parts.at[d - 1, pl.ds(0, cols)],
            part_send.at[d - 1],
            part_recv.at[d - 1],
            (f, (y + d) % reps),
        ).wait()

    @pl.loop(0, owners)
    def _(o):
        col = pick_ref[home, o]
        total = mine[col].astype(f32)
        for d in range(reps - 1):
            total = total + parts[d, col].astype(f32)
        outbox[o] = total.astype(bf16)
        target = g_land.at[
            pl.ds(pl.multiple_of(place * rows, rows), rows),
            pl.ds(pl.multiple_of(y * lane, lane), lane),
        ]
        here = own_plane & (o == f)

        @pl.when(jnp.logical_not(here))
        def _():
            remote(outbox.at[o], target, out_send, out_recv, (o, home)).start()

        @pl.when(here)
        def _():
            pltpu.make_async_copy(outbox.at[o], target, out_recv).start()

    for load in loads[1:]:
        load.wait()
    pltpu.make_async_copy(g_land, g_land, out_recv).wait()
    g_copy = pltpu.make_async_copy(g_land, g_out_ref, g_sem)
    g_copy.start()

    half = jnp.dot(left_root[...], g_land[...], preferred_element_type=f32).astype(bf16)
    conditioned[...] = jnp.dot(half, right_root[...], preferred_element_type=f32)
    gradient = g_land[...].astype(f32)
    moment_new = graft_decay * moment[...] + (1.0 - graft_decay) * gradient * gradient
    adam_step = gradient / (jnp.sqrt(moment_new) + adam_epsilon)
    count = float(block * block)
    adam_mean = jnp.sum(adam_step * adam_step) / count
    cond = conditioned[...]
    cond_mean = jnp.sum(cond * cond) / count
    ratio = (adam_mean + graft_epsilon) / (cond_mean + graft_epsilon)
    scale = jnp.sqrt(jnp.full((1, 1), ratio, f32))
    for q in range(reps):
        quarter = conditioned[:, q * lane : (q + 1) * lane]
        stepped[q] = (scale * quarter).astype(bf16)

    for d in range(1, reps):
        peer = (y + d) % reps
        remote(
            stepped.at[peer],
            relay.at[d - 1],
            relay_send.at[d - 1],
            relay_recv.at[d - 1],
            (f, peer),
        ).start()

    def send_back(source, row):
        @pl.loop(0, per_row)
        def _(i):
            piece = source.at[pl.ds(pl.multiple_of(i * rows, rows), rows)]
            there = row * per_row + i
            here = there == f

            @pl.when(jnp.logical_not(here))
            def _():
                remote(piece, arrived.at[f], back_send, back_recv, (there, y)).start()

            @pl.when(here)
            def _():
                pltpu.make_async_copy(piece, arrived.at[f], back_recv).start()

    send_back(stepped.at[y], y)
    for d in (1, 3, 2):
        remote(
            stepped.at[(y + d) % reps],
            relay.at[d - 1],
            relay_send.at[d - 1],
            relay_recv.at[d - 1],
            (f, (y + d) % reps),
        ).wait_recv()
        send_back(relay.at[d - 1], (y + reps - d) % reps)

    pltpu.make_async_copy(arrived, arrived, back_recv).wait()

    @pl.loop(0, cols)
    def _(c):
        chosen[y, c] = arrived[owner_ref[home, c]]

    for d in range(1, reps):
        remote(
            chosen.at[y],
            chosen.at[y],
            choice_send.at[d - 1],
            choice_recv.at[d - 1],
            (f, (y + d) % reps),
        ).start()

    def place_quarter(q):
        @pl.loop(0, cols)
        def _(c):
            start = pl.multiple_of(c * block + q * lane, lane)
            direction_ref[:, pl.ds(start, lane)] = chosen[q, c]

    place_quarter(y)
    for d in (1, 3, 2):
        source = (y + reps - d) % reps
        remote(
            chosen.at[source],
            chosen.at[source],
            choice_send.at[d - 1],
            choice_recv.at[d - 1],
            (f, (y + d) % reps),
        ).wait_recv()
        place_quarter(source)

    for d in range(1, reps):
        remote(
            chosen.at[y],
            chosen.at[y],
            choice_send.at[d - 1],
            choice_recv.at[d - 1],
            (f, (y + d) % reps),
        ).wait_send()
        remote(
            stepped.at[(y + d) % reps],
            relay.at[d - 1],
            relay_send.at[d - 1],
            relay_recv.at[d - 1],
            (f, (y + d) % reps),
        ).wait_send()
    g_copy.wait()
    sent = outbox.at[pl.ds(0, owners - 1)]
    pltpu.make_async_copy(sent, sent, out_send).wait()

    @pl.when(jnp.logical_not(own_plane))
    def _():
        last = outbox.at[owners - 1]
        pltpu.make_async_copy(last, last, out_send).wait()

    gone = arrived.at[pl.ds(0, owners - 1)]
    pltpu.make_async_copy(gone, gone, back_send).wait()


def local(replica_grads, block_owner, left_factor, right_factor, left_root, right_root, moment):
    owners = lax.axis_size("fsdp")
    reps = lax.axis_size("rep")
    rows, width = replica_grads.shape[1:]
    block = left_factor.shape[4]
    cols = width // block
    lane = block // reps
    per_row = block // rows
    sizes = (owners, reps, cols, rows, block, lane, per_row)

    columns = jnp.arange(cols, dtype=jnp.int32)
    match = block_owner[:, :, None] == jnp.arange(owners, dtype=jnp.int32)[None, None, :]
    pick = jnp.min(jnp.where(match, columns[None, :, None], cols), axis=1)

    any_space = pl.BlockSpec(memory_space=pl.ANY)
    direction, g = pl.pallas_call(
        functools.partial(kernel, sizes),
        out_shape=(
            jax.ShapeDtypeStruct((rows, width), bf16),
            jax.ShapeDtypeStruct((block, block), bf16),
        ),
        in_specs=[pl.BlockSpec(memory_space=pltpu.SMEM)] * 2 + [any_space] * 4,
        out_specs=(pl.BlockSpec(memory_space=pltpu.VMEM), any_space),
        scratch_shapes=[
            pltpu.VMEM((rows, width), bf16),
            pltpu.VMEM((block, block), bf16),
            pltpu.VMEM((block, block), bf16),
            pltpu.VMEM((block, block), f32),
            pltpu.VMEM((reps - 1, cols, rows, lane), bf16),
            pltpu.VMEM((cols + 1, rows, lane), bf16),
            pltpu.VMEM((reps - 1, cols + 1, rows, lane), bf16),
            pltpu.VMEM((owners, rows, lane), bf16),
            pltpu.VMEM((block, block), bf16),
            pltpu.VMEM((block, block), f32),
            pltpu.VMEM((reps, block, lane), bf16),
            pltpu.VMEM((reps - 1, block, lane), bf16),
            pltpu.VMEM((owners, rows, lane), bf16),
            pltpu.VMEM((reps, cols, rows, lane), bf16),
            pltpu.SemaphoreType.DMA((4,)),
            pltpu.SemaphoreType.DMA((reps - 1,)),
            pltpu.SemaphoreType.DMA((reps - 1,)),
            pltpu.SemaphoreType.DMA,
            pltpu.SemaphoreType.DMA,
            pltpu.SemaphoreType.DMA((reps - 1,)),
            pltpu.SemaphoreType.DMA((reps - 1,)),
            pltpu.SemaphoreType.DMA,
            pltpu.SemaphoreType.DMA,
            pltpu.SemaphoreType.DMA((reps - 1,)),
            pltpu.SemaphoreType.DMA((reps - 1,)),
            pltpu.SemaphoreType.DMA,
        ],
        compiler_params=pltpu.CompilerParams(
            collective_id=0, has_side_effects=True, vmem_limit_bytes=40 * 1024 * 1024
        ),
    )(
        pick,
        block_owner,
        replica_grads.reshape(rows, width),
        left_root.reshape(block, block),
        right_root.reshape(block, block),
        moment.reshape(block, block),
    )

    def gram(old, contract):
        product = lax.dot_general(
            g, g, (((contract,), (contract,)), ((), ())), preferred_element_type=f32
        )
        return stat_decay * old.reshape(block, block) + (1.0 - stat_decay) * product

    left_new = gram(left_factor, 1)
    right_new = gram(right_factor, 0)
    g_wide = g.astype(f32)
    moment_new = graft_decay * moment.reshape(block, block) + (1.0 - graft_decay) * g_wide * g_wide
    state_shape = left_factor.shape
    return (
        direction,
        left_new.reshape(state_shape),
        right_new.reshape(state_shape),
        moment_new.reshape(state_shape),
    )


def solution(mesh):
    state = P("fsdp", "rep", None, None, None)
    return jax.shard_map(
        local,
        mesh=mesh,
        in_specs=(P("rep", "fsdp", None), P(), state, state, state, state, state),
        out_specs=(P("fsdp", None), state, state, state),
        check_vma=False,
    )
```

```python
import functools

import jax
import jax.numpy as jnp
from jax import lax
from jax.experimental import pallas as pl
from jax.experimental.pallas import tpu as pltpu
from jax.sharding import PartitionSpec as P

MESH = pl.DeviceIdType.MESH

stat_decay = 0.9
graft_decay = 0.99
adam_epsilon = 1e-08
graft_epsilon = 1e-06

bf16 = jnp.bfloat16
f32 = jnp.float32

cores, xs = 2, 4
halves = 2


def remote(src, dst, send_sem, recv_sem, where):
    return pltpu.make_async_remote_copy(
        src_ref=src,
        dst_ref=dst,
        send_sem=send_sem,
        recv_sem=recv_sem,
        device_id=where,
        device_id_type=MESH,
    )


def settle(ref, sem):
    pltpu.make_async_copy(ref, ref, sem).wait()


def greet(sem, to_f, to_y):
    pl.semaphore_signal(sem, inc=1, device_id=(to_f, to_y), device_id_type=MESH)


def kernel(
    sizes,
    owner_hbm,
    grads_hbm,
    left_root_hbm,
    right_root_hbm,
    left_hbm,
    right_hbm,
    moment_hbm,
    direction_ref,
    left_new_ref,
    right_new_ref,
    moment_new_ref,
    owner,
    pick_row,
    pick,
    grads,
    left_root,
    right_root,
    left,
    right,
    moment,
    stage,
    mine,
    parts,
    outbox,
    g_land,
    conditioned,
    stepped,
    relay,
    arrived,
    chosen,
    load_sem,
    pick_sem,
    part_send,
    part_recv,
    out_send,
    out_recv,
    relay_send,
    relay_recv,
    back_send,
    back_recv,
    choice_send,
    choice_recv,
    *round_sems,
):
    owners, reps, cols, rows, block, lane, per_row = sizes
    half_rows = rows // halves
    f = lax.axis_index("fsdp")
    y = lax.axis_index("rep")
    home = f // per_row
    place = f % per_row
    own_plane = home == y

    def replica(d):
        return (y + d + reps) % reps

    loads = [
        pltpu.make_async_copy(source, target, load_sem.at[number])
        for number, (source, target) in enumerate(
            (
                (grads_hbm, grads),
                (owner_hbm, owner),
                (left_root_hbm, left_root),
                (right_root_hbm, right_root),
                (moment_hbm, moment),
                (left_hbm, left),
                (right_hbm, right),
            )
        )
    ]
    for load in loads:
        load.start()

    zs = owners // (cores * xs)
    core, x, z = f % cores, f // cores % xs, f // (cores * xs)

    def at(dz, dx, dcore):
        return (((z + dz + zs) % zs) * xs + (x + dx + xs) % xs) * cores + (core + dcore) % cores

    near = [(f, replica(d)) for d in range(1, reps)]
    near += [(at(1, 0, 0), y), (at(-1, 0, 0), y), (at(0, 1, 0), y), (at(0, -1, 0), y), (at(0, 0, 1), y)]
    rounds = (
        [(at(1, 0, 0), y), (at(-1, 0, 0), y), (at(0, 1, 0), y), (at(0, -1, 0), y)],
        [(at(2, 0, 0), y), (at(-2, 0, 0), y)],
        [(at(0, 1, 0), y), (at(0, 2, 0), y), (at(0, 3, 0), y)],
        [(at(0, 0, 1), y)],
        [(f, replica(d)) for d in range(1, reps)],
    )
    barrier = pltpu.get_barrier_semaphore()
    for where in near:
        greet(barrier, *where)

    def quarter_of(h, q, c):
        start = pl.multiple_of(c * block + q * lane, lane)
        return grads[h * half_rows : (h + 1) * half_rows, pl.ds(start, lane)]

    loads[0].wait()
    for h in range(halves):
        for d in range(1, reps):
            peer = replica(d)

            @pl.loop(0, cols)
            def _(c):
                stage[h, d - 1, c] = quarter_of(h, peer, c)

        @pl.loop(0, cols)
        def _(c):
            mine[h, c] = quarter_of(h, y, c)

        nothing = jnp.zeros((half_rows, lane), bf16)
        mine[h, cols] = nothing
        for d in range(1, reps):
            parts[h][d - 1, cols] = nothing

    loads[1].wait()
    owner_of_lane = lax.broadcasted_iota(jnp.int32, pick_row.shape, 1)
    picked = jnp.full(pick_row.shape, cols, jnp.int32)
    for c in range(cols):
        picked = jnp.where(owner_of_lane == owner[home, c], c, picked)
    pick_row[...] = picked
    pick_copy = pltpu.make_async_copy(pick_row, pick, pick_sem)
    pick_copy.start()
    pick_copy.wait()

    def part_copy(h, d):
        return remote(
            stage.at[h, d - 1],
            parts[h].at[d - 1, pl.ds(0, cols)],
            part_send.at[h, d - 1],
            part_recv.at[h, d - 1],
            (f, replica(d)),
        )

    pl.semaphore_wait(barrier, len(near))
    for h in range(halves):
        for d in (2, 1, 3):
            part_copy(h, d).start()
    for number, peers in enumerate(rounds):
        for where in peers:
            greet(round_sems[number], *where)
        pl.semaphore_wait(round_sems[number], len(peers))

    for h in range(halves):
        for d in (1, 3, 2):
            part_copy(h, d).wait_recv()
        row_start = pl.multiple_of(place * rows + h * half_rows, half_rows)
        target = g_land.at[
            pl.ds(row_start, half_rows), pl.ds(pl.multiple_of(y * lane, lane), lane)
        ]

        @pl.loop(0, owners)
        def _(o):
            col = pick[0, o]
            total = mine[h, col].astype(f32)
            for d in range(reps - 1):
                total = total + parts[h][d, col].astype(f32)
            outbox[h, o] = total.astype(bf16)
            here = own_plane & (o == f)

            @pl.when(jnp.logical_not(here))
            def _():
                remote(
                    outbox.at[h, o], target, out_send.at[h], out_recv.at[h], (o, home)
                ).start()

            @pl.when(here)
            def _():
                pltpu.make_async_copy(outbox.at[h, o], target, out_recv.at[h]).start()

    for load in loads[2:]:
        load.wait()
    for h in range(halves):
        settle(arrived[h], out_recv.at[h])

    half = jnp.dot(left_root[...], g_land[...], preferred_element_type=f32).astype(bf16)
    conditioned[...] = jnp.dot(half, right_root[...], preferred_element_type=f32)
    gradient = g_land[...].astype(f32)
    moment_new = graft_decay * moment[...] + (1.0 - graft_decay) * gradient * gradient
    moment_new_ref[...] = moment_new
    adam_step = gradient / (jnp.sqrt(moment_new) + adam_epsilon)
    count = float(block * block)
    adam_mean = jnp.sum(adam_step * adam_step) / count
    cond = conditioned[...]
    cond_mean = jnp.sum(cond * cond) / count
    ratio = (adam_mean + graft_epsilon) / (cond_mean + graft_epsilon)
    scale = jnp.sqrt(jnp.full((1, 1), ratio, f32))
    for q in range(reps):
        quarter = (scale * conditioned[:, q * lane : (q + 1) * lane]).astype(bf16)
        quarter = quarter.reshape(per_row, halves, half_rows, lane)
        for h in range(halves):
            stepped[q, h] = quarter[:, h]

    def relay_copy(h, d):
        return remote(
            stepped.at[replica(d), h],
            relay.at[h, d - 1],
            relay_send.at[h, d - 1],
            relay_recv.at[h, d - 1],
            (f, replica(d)),
        )

    for h in range(halves):
        for d in (1, 3, 2):
            relay_copy(h, d).start()

    def send_back(h, source, row):
        @pl.loop(0, per_row)
        def _(i):
            there = row * per_row + i
            here = there == f
            target = arrived[h].at[f]

            @pl.when(jnp.logical_not(here))
            def _():
                remote(
                    source.at[i], target, back_send.at[h], back_recv.at[h], (there, y)
                ).start()

            @pl.when(here)
            def _():
                pltpu.make_async_copy(source.at[i], target, back_recv.at[h]).start()

    for h in range(halves):
        send_back(h, stepped.at[y, h], y)
        for d in (1, 3, 2):
            relay_copy(h, d).wait_recv()
            send_back(h, relay.at[h, d - 1], replica(-d))

    def gram(old, contract):
        product = lax.dot_general(
            g_land[...],
            g_land[...],
            (((contract,), (contract,)), ((), ())),
            preferred_element_type=f32,
        )
        return stat_decay * old[...] + (1.0 - stat_decay) * product

    left_new_ref[...] = gram(left, 1)
    right_new_ref[...] = gram(right, 0)

    def choice_copy(h, d, source):
        return remote(
            chosen.at[h, source],
            chosen.at[h, source],
            choice_send.at[h, d - 1],
            choice_recv.at[h, d - 1],
            (f, replica(d)),
        )

    for h in range(halves):
        settle(arrived[h], back_recv.at[h])

        @pl.loop(0, cols)
        def _(c):
            chosen[h, y, c] = arrived[h][owner[home, c]]

        for d in (2, 1, 3):
            choice_copy(h, d, y).start()

    def place_quarter(h, q):
        @pl.loop(0, cols)
        def _(c):
            start = pl.multiple_of(c * block + q * lane, lane)
            direction_ref[h * half_rows : (h + 1) * half_rows, pl.ds(start, lane)] = chosen[h, q, c]

    for h in range(halves):
        place_quarter(h, y)
        for d in (1, 3, 2):
            choice_copy(h, d, replica(-d)).wait_recv()
            place_quarter(h, replica(-d))

    for h in range(halves):
        for d in range(1, reps):
            part_copy(h, d).wait_send()
            relay_copy(h, d).wait_send()
            choice_copy(h, d, y).wait_send()
        settle(outbox.at[h, pl.ds(0, owners - 1)], out_send.at[h])

        @pl.when(jnp.logical_not(own_plane))
        def _():
            settle(outbox.at[h, owners - 1], out_send.at[h])

        settle(arrived[h].at[pl.ds(0, owners - 1)], back_send.at[h])


def local(replica_grads, block_owner, left_factor, right_factor, left_root, right_root, moment):
    owners = lax.axis_size("fsdp")
    reps = lax.axis_size("rep")
    rows, width = replica_grads.shape[1:]
    block = left_factor.shape[4]
    cols = width // block
    lane = block // reps
    per_row = block // rows
    half_rows = rows // halves
    sizes = (owners, reps, cols, rows, block, lane, per_row)

    hbm = pl.BlockSpec(memory_space=pltpu.HBM)
    vmem = pl.BlockSpec(memory_space=pltpu.VMEM)
    square = jax.ShapeDtypeStruct((block, block), f32)
    results = (jax.ShapeDtypeStruct((rows, width), bf16), square, square, square)
    others = reps - 1
    by_half = pltpu.SemaphoreType.DMA((halves,))
    by_peer = pltpu.SemaphoreType.DMA((halves, others))
    flat = [
        array.reshape(block, block)
        for array in (left_root, right_root, left_factor, right_factor, moment)
    ]
    outs = pl.pallas_call(
        functools.partial(kernel, sizes),
        out_shape=results,
        in_specs=[hbm] * 7,
        out_specs=(vmem,) * 4,
        scratch_shapes=[
            pltpu.SMEM(block_owner.shape, jnp.int32),
            pltpu.VMEM((8, 128), jnp.int32),
            pltpu.SMEM((8, 128), jnp.int32),
            pltpu.VMEM((rows, width), bf16),
            pltpu.VMEM((block, block), bf16),
            pltpu.VMEM((block, block), bf16),
            pltpu.VMEM((block, block), f32),
            pltpu.VMEM((block, block), f32),
            pltpu.VMEM((block, block), f32),
            pltpu.VMEM((halves, others, cols, half_rows, lane), bf16),
            pltpu.VMEM((halves, cols + 1, half_rows, lane), bf16),
            [pltpu.VMEM((others, cols + 1, half_rows, lane), bf16)] * halves,
            pltpu.VMEM((halves, owners, half_rows, lane), bf16),
            pltpu.VMEM((block, block), bf16),
            pltpu.VMEM((block, block), f32),
            pltpu.VMEM((reps, halves, per_row, half_rows, lane), bf16),
            pltpu.VMEM((halves, others, per_row, half_rows, lane), bf16),
            [pltpu.VMEM((owners, half_rows, lane), bf16)] * halves,
            pltpu.VMEM((halves, reps, cols, half_rows, lane), bf16),
            pltpu.SemaphoreType.DMA((7,)),
            pltpu.SemaphoreType.DMA,
            by_peer,
            by_peer,
            by_half,
            by_half,
            by_peer,
            by_peer,
            by_half,
            by_half,
            by_peer,
            by_peer,
        ]
        + [pltpu.SemaphoreType.REGULAR] * 5,
        compiler_params=pltpu.CompilerParams(
            collective_id=0, has_side_effects=True, vmem_limit_bytes=24 * 1024 * 1024
        ),
    )(
        *(
            pltpu.with_memory_space_constraint(array, pltpu.HBM)
            for array in (block_owner, replica_grads.reshape(rows, width), *flat)
        )
    )

    direction, left_new, right_new, moment_new = outs
    state_shape = left_factor.shape
    return (
        direction,
        left_new.reshape(state_shape),
        right_new.reshape(state_shape),
        moment_new.reshape(state_shape),
    )


def solution(mesh):
    state = P("fsdp", "rep", None, None, None)
    return jax.shard_map(
        local,
        mesh=mesh,
        in_specs=(P("rep", "fsdp", None), P(), state, state, state, state, state),
        out_specs=(P("fsdp", None), state, state, state),
        check_vma=False,
    )
```

```python
import functools

import jax
import jax.numpy as jnp
from jax import lax
from jax.experimental import pallas as pl
from jax.experimental.pallas import tpu as pltpu
from jax.sharding import PartitionSpec as P

MESH = pl.DeviceIdType.MESH

stat_decay = 0.9
graft_decay = 0.99
adam_epsilon = 1e-08
graft_epsilon = 1e-06

bf16 = jnp.bfloat16
f32 = jnp.float32

cores, xs = 2, 4
halves = 2
ways = (1, -1)


def remote(src, dst, send_sem, recv_sem, where):
    return pltpu.make_async_remote_copy(
        src_ref=src,
        dst_ref=dst,
        send_sem=send_sem,
        recv_sem=recv_sem,
        device_id=where,
        device_id_type=MESH,
    )


def settle(ref, sem):
    pltpu.make_async_copy(ref, ref, sem).wait()


def greet(sem, to_f, to_y):
    pl.semaphore_signal(sem, inc=1, device_id=(to_f, to_y), device_id_type=MESH)


def kernel(
    sizes,
    owner_hbm,
    grads_hbm,
    left_root_hbm,
    right_root_hbm,
    left_hbm,
    right_hbm,
    moment_hbm,
    direction_ref,
    left_new_ref,
    right_new_ref,
    moment_new_ref,
    owner,
    pick_row,
    pick,
    grads,
    left_root,
    right_root,
    left,
    right,
    moment,
    stage,
    mine,
    via,
    parts,
    outbox,
    g_land,
    conditioned,
    stepped,
    relay,
    arrived,
    chosen,
    load_sem,
    pick_sem,
    part_send,
    part_recv,
    out_send,
    out_recv,
    relay_send,
    relay_recv,
    back_send,
    back_recv,
    choice_send,
    choice_recv,
    *round_sems,
):
    owners, reps, cols, rows, block, lane, per_row = sizes
    half_rows = rows // halves
    f = lax.axis_index("fsdp")
    y = lax.axis_index("rep")
    home = f // per_row
    place = f % per_row
    own_plane = home == y

    def replica(d):
        return (y + d + reps) % reps

    loads = [
        pltpu.make_async_copy(source, target, load_sem.at[number])
        for number, (source, target) in enumerate(
            (
                (grads_hbm, grads),
                (owner_hbm, owner),
                (left_root_hbm, left_root),
                (right_root_hbm, right_root),
                (moment_hbm, moment),
                (left_hbm, left),
                (right_hbm, right),
            )
        )
    ]
    for load in loads:
        load.start()

    zs = owners // (cores * xs)
    core, x, z = f % cores, f // cores % xs, f // (cores * xs)

    def at(dz, dx, dcore):
        return (((z + dz + zs) % zs) * xs + (x + dx + xs) % xs) * cores + (core + dcore) % cores

    replicas = [(f, replica(d)) for d in range(1, reps)]
    along_z = [(at(d, 0, 0), y) for d in range(1, zs)]
    layer = [(at(0, dx, dcore), y) for dx in range(xs) for dcore in range(cores) if dx or dcore]
    near = replicas + along_z + layer
    rounds = (along_z, replicas)
    barrier = pltpu.get_barrier_semaphore()
    for where in near:
        greet(barrier, *where)

    def quarter_of(h, q, c):
        start = pl.multiple_of(c * block + q * lane, lane)
        return grads[h * half_rows : (h + 1) * half_rows, pl.ds(start, lane)]

    loads[0].wait()
    for h in range(halves):
        for d in range(1, reps):
            peer = replica(d)

            @pl.loop(0, cols)
            def _(c):
                stage[h, d - 1, c] = quarter_of(h, peer, c)

        @pl.loop(0, cols)
        def _(c):
            mine[h, c] = quarter_of(h, y, c)

        nothing = jnp.zeros((half_rows, lane), bf16)
        mine[h, cols] = nothing
        for d in range(2):
            parts[h][d, cols] = nothing

    loads[1].wait()
    owner_of_lane = lax.broadcasted_iota(jnp.int32, pick_row.shape, 1)
    picked = jnp.full(pick_row.shape, cols, jnp.int32)
    for c in range(cols):
        picked = jnp.where(owner_of_lane == owner[home, c], c, picked)
    pick_row[...] = picked
    pick_copy = pltpu.make_async_copy(pick_row, pick, pick_sem)
    pick_copy.start()
    pick_copy.wait()

    spans = ((0, (cols + 1) // 2), ((cols + 1) // 2, cols))

    def part_copy(h, side, leg):
        way, (first, last) = ways[side], spans[side]
        span = pl.ds(first, last - first)
        source, target, where = (
            (stage.at[h, 1, span], via.at[h, span], replica(way)),
            (stage.at[h, -way % reps - 1, span], parts[h].at[1, span], replica(-way)),
            (stage.at[h, way % reps - 1, span], parts[h].at[0, span], replica(way)),
        )[leg]
        return remote(
            source, target, part_send.at[h, side, leg], part_recv.at[h, side, leg], (f, where)
        )

    def send_parts(h, leg):
        for side in range(2):
            part_copy(h, side, leg).start()

    def pass_on(h):
        for side in range(2):
            part_copy(h, side, 0).wait_recv()
            slot = ways[side] % reps - 1

            @pl.loop(*spans[side])
            def _(c):
                both = stage[h, slot, c].astype(f32) + via[h, c].astype(f32)
                stage[h, slot, c] = both.astype(bf16)

            part_copy(h, side, 2).start()

    pl.semaphore_wait(barrier, len(near))
    send_parts(0, 0)
    send_parts(1, 0)
    send_parts(0, 1)
    for where in rounds[0]:
        greet(round_sems[0], *where)
    pass_on(0)
    send_parts(1, 1)
    pl.semaphore_wait(round_sems[0], len(rounds[0]))
    for where in rounds[1]:
        greet(round_sems[1], *where)
    pass_on(1)
    pl.semaphore_wait(round_sems[1], len(rounds[1]))

    for h in range(halves):
        for leg in (1, 2):
            for side in range(2):
                part_copy(h, side, leg).wait_recv()
        row_start = pl.multiple_of(place * rows + h * half_rows, half_rows)
        target = g_land.at[
            pl.ds(row_start, half_rows), pl.ds(pl.multiple_of(y * lane, lane), lane)
        ]

        @pl.loop(0, owners)
        def _(o):
            col = pick[0, o]
            total = mine[h, col].astype(f32)
            for d in range(2):
                total = total + parts[h][d, col].astype(f32)
            outbox[h, o] = total.astype(bf16)
            here = own_plane & (o == f)

            @pl.when(jnp.logical_not(here))
            def _():
                remote(
                    outbox.at[h, o], target, out_send.at[h], out_recv.at[h], (o, home)
                ).start()

            @pl.when(here)
            def _():
                pltpu.make_async_copy(outbox.at[h, o], target, out_recv.at[h]).start()

    for load in loads[2:]:
        load.wait()
    for h in range(halves):
        settle(arrived[h], out_recv.at[h])

    half = jnp.dot(left_root[...], g_land[...], preferred_element_type=f32).astype(bf16)
    conditioned[...] = jnp.dot(half, right_root[...], preferred_element_type=f32)
    gradient = g_land[...].astype(f32)
    moment_new = graft_decay * moment[...] + (1.0 - graft_decay) * gradient * gradient
    moment_new_ref[...] = moment_new
    adam_step = gradient / (jnp.sqrt(moment_new) + adam_epsilon)
    count = float(block * block)
    adam_mean = jnp.sum(adam_step * adam_step) / count
    cond = conditioned[...]
    cond_mean = jnp.sum(cond * cond) / count
    ratio = (adam_mean + graft_epsilon) / (cond_mean + graft_epsilon)
    scale = jnp.sqrt(jnp.full((1, 1), ratio, f32))
    for q in range(reps):
        quarter = (scale * conditioned[:, q * lane : (q + 1) * lane]).astype(bf16)
        quarter = quarter.reshape(per_row, halves, half_rows, lane)
        for h in range(halves):
            stepped[q, h] = quarter[:, h]

    def relay_copy(h, d):
        return remote(
            stepped.at[replica(d), h],
            relay.at[h, d],
            relay_send.at[h, d - 1],
            relay_recv.at[h, d - 1],
            (f, replica(d)),
        )

    for h in range(halves):
        for d in (1, 3, 2):
            relay_copy(h, d).start()

    def send_back(h):
        @pl.loop(0, owners)
        def _(there):
            row = there // per_row
            source = relay.at[h, (y - row + reps) % reps, there % per_row]
            here = there == f
            target = arrived[h].at[f]

            @pl.when(jnp.logical_not(here))
            def _():
                remote(source, target, back_send.at[h], back_recv.at[h], (there, y)).start()

            @pl.when(here)
            def _():
                pltpu.make_async_copy(source, target, back_recv.at[h]).start()

    for h in range(halves):
        relay[h, 0] = stepped[y, h]
        for d in (1, 3, 2):
            relay_copy(h, d).wait_recv()
        send_back(h)

    def gram(old, contract):
        product = lax.dot_general(
            g_land[...],
            g_land[...],
            (((contract,), (contract,)), ((), ())),
            preferred_element_type=f32,
        )
        return stat_decay * old[...] + (1.0 - stat_decay) * product

    left_new_ref[...] = gram(left, 1)
    right_new_ref[...] = gram(right, 0)

    def choice_copy(h, leg):
        every = pl.ds(0, cols)
        spread = [pl.ds(first, last - first) for first, last in spans]
        source, span, where = (
            (y, every, replica(1)),
            (y, every, replica(-1)),
            (replica(-1), spread[0], replica(1)),
            (replica(1), spread[1], replica(-1)),
        )[leg]
        piece = chosen.at[h, source, span]
        return remote(piece, piece, choice_send.at[h, leg], choice_recv.at[h, leg], (f, where))

    for h in range(halves):
        settle(arrived[h], back_recv.at[h])

        @pl.loop(0, cols)
        def _(c):
            chosen[h, y, c] = arrived[h][owner[home, c]]

        for leg in (0, 1):
            choice_copy(h, leg).start()

    def place_quarter(h, q):
        @pl.loop(0, cols)
        def _(c):
            start = pl.multiple_of(c * block + q * lane, lane)
            direction_ref[h * half_rows : (h + 1) * half_rows, pl.ds(start, lane)] = chosen[h, q, c]

    for h in range(halves):
        for leg in (0, 1):
            choice_copy(h, leg).wait_recv()
            choice_copy(h, leg + 2).start()
    for h in range(halves):
        for d in (0, -1, 1):
            place_quarter(h, replica(d))
    for h in range(halves):
        for leg in (2, 3):
            choice_copy(h, leg).wait_recv()
        place_quarter(h, replica(2))

    for h in range(halves):
        for d in range(1, reps):
            for side in range(2):
                part_copy(h, side, d - 1).wait_send()
            relay_copy(h, d).wait_send()
        for leg in range(4):
            choice_copy(h, leg).wait_send()
        settle(outbox.at[h, pl.ds(0, owners - 1)], out_send.at[h])

        @pl.when(jnp.logical_not(own_plane))
        def _():
            settle(outbox.at[h, owners - 1], out_send.at[h])

        settle(arrived[h].at[pl.ds(0, owners - 1)], back_send.at[h])


def finish(*refs):
    count = len(refs) // 2
    sem = refs[-1]
    copies = [
        pltpu.make_async_copy(refs[i], refs[count + i], sem.at[i]) for i in range(count)
    ]
    for copy in copies:
        copy.start()
    for copy in copies:
        copy.wait()


def local(replica_grads, block_owner, left_factor, right_factor, left_root, right_root, moment):
    owners = lax.axis_size("fsdp")
    reps = lax.axis_size("rep")
    rows, width = replica_grads.shape[1:]
    block = left_factor.shape[4]
    cols = width // block
    lane = block // reps
    per_row = block // rows
    half_rows = rows // halves
    sizes = (owners, reps, cols, rows, block, lane, per_row)

    hbm = pl.BlockSpec(memory_space=pltpu.HBM)
    vmem = pl.BlockSpec(memory_space=pltpu.VMEM)
    square = jax.ShapeDtypeStruct((block, block), f32)
    results = (jax.ShapeDtypeStruct((rows, width), bf16), square, square, square)
    others = reps - 1
    by_half = pltpu.SemaphoreType.DMA((halves,))
    by_peer = pltpu.SemaphoreType.DMA((halves, others))
    by_side = pltpu.SemaphoreType.DMA((halves, 2, 3))
    by_leg = pltpu.SemaphoreType.DMA((halves, 4))
    flat = [
        array.reshape(block, block)
        for array in (left_root, right_root, left_factor, right_factor, moment)
    ]
    outs = pl.pallas_call(
        functools.partial(kernel, sizes),
        out_shape=results,
        in_specs=[hbm] * 7,
        out_specs=(vmem,) * 4,
        scratch_shapes=[
            pltpu.SMEM(block_owner.shape, jnp.int32),
            pltpu.VMEM((8, 128), jnp.int32),
            pltpu.SMEM((8, 128), jnp.int32),
            pltpu.VMEM((rows, width), bf16),
            pltpu.VMEM((block, block), bf16),
            pltpu.VMEM((block, block), bf16),
            pltpu.VMEM((block, block), f32),
            pltpu.VMEM((block, block), f32),
            pltpu.VMEM((block, block), f32),
            pltpu.VMEM((halves, others, cols, half_rows, lane), bf16),
            pltpu.VMEM((halves, cols + 1, half_rows, lane), bf16),
            pltpu.VMEM((halves, cols, half_rows, lane), bf16),
            [pltpu.VMEM((2, cols + 1, half_rows, lane), bf16)] * halves,
            pltpu.VMEM((halves, owners, half_rows, lane), bf16),
            pltpu.VMEM((block, block), bf16),
            pltpu.VMEM((block, block), f32),
            pltpu.VMEM((reps, halves, per_row, half_rows, lane), bf16),
            pltpu.VMEM((halves, reps, per_row, half_rows, lane), bf16),
            [pltpu.VMEM((owners, half_rows, lane), bf16)] * halves,
            pltpu.VMEM((halves, reps, cols, half_rows, lane), bf16),
            pltpu.SemaphoreType.DMA((7,)),
            pltpu.SemaphoreType.DMA,
            by_side,
            by_side,
            by_half,
            by_half,
            by_peer,
            by_peer,
            by_half,
            by_half,
            by_leg,
            by_leg,
        ]
        + [pltpu.SemaphoreType.REGULAR] * 2,
        compiler_params=pltpu.CompilerParams(
            collective_id=0, has_side_effects=True, vmem_limit_bytes=24 * 1024 * 1024
        ),
    )(
        *(
            pltpu.with_memory_space_constraint(array, pltpu.HBM)
            for array in (block_owner, replica_grads.reshape(rows, width), *flat)
        )
    )

    direction, left_new, right_new, moment_new = pl.pallas_call(
        finish,
        out_shape=results,
        in_specs=[vmem] * 4,
        out_specs=(hbm,) * 4,
        scratch_shapes=[pltpu.SemaphoreType.DMA((4,))],
        compiler_params=pltpu.CompilerParams(vmem_limit_bytes=1024*1024),
    )(*(pltpu.with_memory_space_constraint(array, pltpu.VMEM) for array in outs))
    state_shape = left_factor.shape
    return (
        direction,
        left_new.reshape(state_shape),
        right_new.reshape(state_shape),
        moment_new.reshape(state_shape),
    )


def solution(mesh):
    state = P("fsdp", "rep", None, None, None)
    return jax.shard_map(
        local,
        mesh=mesh,
        in_specs=(P("rep", "fsdp", None), P(), state, state, state, state, state),
        out_specs=(P("fsdp", None), state, state, state),
        check_vma=False,
    )
```

```python
import functools

import jax
import jax.numpy as jnp
from jax import lax
from jax.experimental import pallas as pl
from jax.experimental.pallas import tpu as pltpu
from jax.sharding import PartitionSpec as P

MESH = pl.DeviceIdType.MESH

stat_decay = 0.9
graft_decay = 0.99
adam_epsilon = 1e-08
graft_epsilon = 1e-06

bf16 = jnp.bfloat16
f32 = jnp.float32

cores, xs = 2, 4
halves = 2
ways = (1, -1)


def remote(src, dst, send_sem, recv_sem, where):
    return pltpu.make_async_remote_copy(
        src_ref=src,
        dst_ref=dst,
        send_sem=send_sem,
        recv_sem=recv_sem,
        device_id=where,
        device_id_type=MESH,
    )


def settle(ref, sem):
    pltpu.make_async_copy(ref, ref, sem).wait()


def greet(sem, to_f, to_y):
    pl.semaphore_signal(sem, inc=1, device_id=(to_f, to_y), device_id_type=MESH)


def kernel(
    sizes,
    owner_hbm,
    grads_hbm,
    left_root_hbm,
    right_root_hbm,
    left_hbm,
    right_hbm,
    moment_hbm,
    direction_ref,
    left_new_ref,
    right_new_ref,
    moment_new_ref,
    owner,
    pick_row,
    pick,
    grads,
    left_root,
    right_root,
    left,
    right,
    moment,
    stage,
    mine,
    via,
    parts,
    outbox,
    g_land,
    conditioned,
    stepped,
    relay,
    arrived,
    chosen,
    load_sem,
    pick_sem,
    part_send,
    part_recv,
    out_send,
    out_recv,
    relay_send,
    relay_recv,
    back_send,
    back_recv,
    choice_send,
    choice_recv,
    *round_sems,
):
    owners, reps, cols, rows, block, lane, per_row = sizes
    half_rows = rows // halves
    f = lax.axis_index("fsdp")
    y = lax.axis_index("rep")
    home = f // per_row
    place = f % per_row
    own_plane = home == y

    def replica(d):
        return (y + d + reps) % reps

    loads = [
        pltpu.make_async_copy(source, target, load_sem.at[number])
        for number, (source, target) in enumerate(
            (
                (grads_hbm, grads),
                (owner_hbm, owner),
                (left_root_hbm, left_root),
                (right_root_hbm, right_root),
                (moment_hbm, moment),
                (left_hbm, left),
                (right_hbm, right),
            )
        )
    ]
    for load in loads[:2]:
        load.start()

    zs = owners // (cores * xs)
    core, x, z = f % cores, f // cores % xs, f // (cores * xs)

    def at(dz, dx, dcore):
        return (((z + dz + zs) % zs) * xs + (x + dx + xs) % xs) * cores + (core + dcore) % cores

    replicas = [(f, replica(d)) for d in range(1, reps)]
    close = [(at(d, 0, 0), y) for d in (1, -1, 2, -2)]
    layer = [(at(0, dx, dcore), y) for dx in range(xs) for dcore in range(cores) if dx or dcore]
    near = replicas + close + layer
    rounds = (close, close[2:], replicas)
    barrier = pltpu.get_barrier_semaphore()
    for where in near:
        greet(barrier, *where)

    def set_out(d):
        for h in range(halves):

            @pl.loop(0, cols, unroll=True)
            def _(c):
                start = pl.multiple_of(c * block + replica(d) * lane, lane)
                piece = grads[h * half_rows : (h + 1) * half_rows, pl.ds(start, lane)]
                if d:
                    stage[h, d - 1, c] = piece
                else:
                    mine[h, c] = piece

    loads[0].wait()
    set_out(2)

    spans = ((0, (cols + 1) // 2), ((cols + 1) // 2, cols))

    def part_copy(h, side, leg):
        way, (first, last) = ways[side], spans[side]
        span = pl.ds(first, last - first)
        source, target, where = (
            (stage.at[h, 1, span], via.at[h, span], replica(way)),
            (stage.at[h, -way % reps - 1, span], parts[h].at[1, span], replica(-way)),
            (stage.at[h, way % reps - 1, span], parts[h].at[0, span], replica(way)),
        )[leg]
        return remote(
            source, target, part_send.at[h, side, leg], part_recv.at[h, side, leg], (f, where)
        )

    def send_parts(h, leg):
        for side in range(2):
            part_copy(h, side, leg).start()

    def pass_on(h):
        for side in range(2):
            part_copy(h, side, 0).wait_recv()
            slot = ways[side] % reps - 1

            @pl.loop(*spans[side], unroll=True)
            def _(c):
                both = stage[h, slot, c].astype(f32) + via[h, c].astype(f32)
                stage[h, slot, c] = both.astype(bf16)

            part_copy(h, side, 2).start()

    pl.semaphore_wait(barrier, len(near))
    send_parts(0, 0)
    send_parts(1, 0)
    set_out(1)
    set_out(3)
    send_parts(0, 1)
    for where in rounds[0]:
        greet(round_sems[0], *where)
    for load in loads[2:]:
        load.start()
    set_out(0)
    for h in range(halves):
        nothing = jnp.zeros((half_rows, lane), bf16)
        mine[h, cols] = nothing
        for d in range(2):
            parts[h][d, cols] = nothing

    loads[1].wait()
    owner_of_lane = lax.broadcasted_iota(jnp.int32, pick_row.shape, 1)
    picked = jnp.full(pick_row.shape, cols, jnp.int32)
    for c in range(cols):
        picked = jnp.where(owner_of_lane == owner[home, c], c, picked)
    pick_row[...] = picked
    pick_copy = pltpu.make_async_copy(pick_row, pick, pick_sem)
    pick_copy.start()
    pick_copy.wait()

    pl.semaphore_wait(round_sems[0], len(rounds[0]))
    for where in rounds[1]:
        greet(round_sems[1], *where)
    pass_on(0)
    send_parts(1, 1)
    pl.semaphore_wait(round_sems[1], len(rounds[1]))
    for where in rounds[2]:
        greet(round_sems[2], *where)
    pass_on(1)
    pl.semaphore_wait(round_sems[2], len(rounds[2]))

    for h in range(halves):
        for leg in (1, 2):
            for side in range(2):
                part_copy(h, side, leg).wait_recv()
        row_start = pl.multiple_of(place * rows + h * half_rows, half_rows)
        target = g_land.at[
            pl.ds(row_start, half_rows), pl.ds(pl.multiple_of(y * lane, lane), lane)
        ]

        @pl.loop(0, owners)
        def _(o):
            col = pick[0, o]
            total = mine[h, col].astype(f32)
            for d in range(2):
                total = total + parts[h][d, col].astype(f32)
            outbox[h, o] = total.astype(bf16)
            here = own_plane & (o == f)

            @pl.when(jnp.logical_not(here))
            def _():
                remote(
                    outbox.at[h, o], target, out_send.at[h], out_recv.at[h], (o, home)
                ).start()

            @pl.when(here)
            def _():
                pltpu.make_async_copy(outbox.at[h, o], target, out_recv.at[h]).start()

    for load in loads[2:]:
        load.wait()
    for h in range(halves):
        settle(arrived[h], out_recv.at[h])

    half = jnp.dot(left_root[...], g_land[...], preferred_element_type=f32).astype(bf16)
    conditioned[...] = jnp.dot(half, right_root[...], preferred_element_type=f32)
    gradient = g_land[...].astype(f32)
    moment_new = graft_decay * moment[...] + (1.0 - graft_decay) * gradient * gradient
    moment_new_ref[...] = moment_new
    adam_step = gradient / (jnp.sqrt(moment_new) + adam_epsilon)
    count = float(block * block)
    adam_mean = jnp.sum(adam_step * adam_step) / count
    cond = conditioned[...]
    cond_mean = jnp.sum(cond * cond) / count
    ratio = (adam_mean + graft_epsilon) / (cond_mean + graft_epsilon)
    scale = jnp.sqrt(jnp.full((1, 1), ratio, f32))
    for q in range(reps):
        quarter = (scale * conditioned[:, q * lane : (q + 1) * lane]).astype(bf16)
        quarter = quarter.reshape(per_row, halves, half_rows, lane)
        for h in range(halves):
            stepped[q, h] = quarter[:, h]

    groups = [(h, j) for h in range(halves) for j in range(2)]
    group_rows = per_row // 2

    def relay_copy(h, j, d):
        span = pl.ds(j * group_rows, group_rows)
        return remote(
            stepped.at[replica(d), h, span],
            relay.at[h, d, span],
            relay_send.at[h, j, d - 1],
            relay_recv.at[h, j, d - 1],
            (f, replica(d)),
        )

    for h, j in groups[:2]:
        for d in (1, 3, 2):
            relay_copy(h, j, d).start()

    def send_back(h, j):
        @pl.loop(0, reps * group_rows)
        def _(k):
            there = k // group_rows * per_row + j * group_rows + k % group_rows
            row = there // per_row
            source = relay.at[h, (y - row + reps) % reps, there % per_row]
            here = there == f
            target = arrived[h].at[f]

            @pl.when(jnp.logical_not(here))
            def _():
                remote(source, target, back_send.at[h], back_recv.at[h], (there, y)).start()

            @pl.when(here)
            def _():
                pltpu.make_async_copy(source, target, back_recv.at[h]).start()

    for h in range(halves):
        relay[h, 0] = stepped[y, h]
    for number, (h, j) in enumerate(groups):
        for d in (1, 3, 2):
            relay_copy(h, j, d).wait_recv()
            if number + 2 < len(groups):
                relay_copy(*groups[number + 2], d).start()
        send_back(h, j)

    def gram(old, contract):
        product = lax.dot_general(
            g_land[...],
            g_land[...],
            (((contract,), (contract,)), ((), ())),
            preferred_element_type=f32,
        )
        return stat_decay * old[...] + (1.0 - stat_decay) * product

    left_new_ref[...] = gram(left, 1)
    right_new_ref[...] = gram(right, 0)

    def choice_copy(h, leg):
        spread = [pl.ds(first, last - first) for first, last in spans]
        source, span, where = (
            (y, spread[0], replica(1)),
            (y, spread[1], replica(-1)),
            (y, spread[1], replica(1)),
            (y, spread[0], replica(-1)),
            (replica(-1), spread[0], replica(1)),
            (replica(1), spread[1], replica(-1)),
        )[leg]
        piece = chosen.at[h, source, span]
        return remote(piece, piece, choice_send.at[h, leg], choice_recv.at[h, leg], (f, where))

    for h in range(halves):
        settle(arrived[h], back_recv.at[h])

        @pl.loop(0, cols, unroll=True)
        def _(c):
            chosen[h, y, c] = arrived[h][owner[home, c]]

        for leg in range(4):
            choice_copy(h, leg).start()

    def place_quarter(h, q):
        @pl.loop(0, cols, unroll=True)
        def _(c):
            start = pl.multiple_of(c * block + q * lane, lane)
            direction_ref[h * half_rows : (h + 1) * half_rows, pl.ds(start, lane)] = chosen[h, q, c]

    for h in range(halves):
        for leg in (0, 1):
            choice_copy(h, leg).wait_recv()
            choice_copy(h, leg + 4).start()
    for h in range(halves):
        place_quarter(h, y)
        for leg in (2, 3):
            choice_copy(h, leg).wait_recv()
        for d in (-1, 1):
            place_quarter(h, replica(d))
    for h in range(halves):
        for leg in (4, 5):
            choice_copy(h, leg).wait_recv()
        place_quarter(h, replica(2))

    for h in range(halves):
        for d in range(1, reps):
            for side in range(2):
                part_copy(h, side, d - 1).wait_send()
            for j in range(2):
                relay_copy(h, j, d).wait_send()
        for leg in range(6):
            choice_copy(h, leg).wait_send()
        settle(outbox.at[h, pl.ds(0, owners - 1)], out_send.at[h])

        @pl.when(jnp.logical_not(own_plane))
        def _():
            settle(outbox.at[h, owners - 1], out_send.at[h])

        settle(arrived[h].at[pl.ds(0, owners - 1)], back_send.at[h])


def finish(*refs):
    count = len(refs) // 2
    sem = refs[-1]
    copies = [
        pltpu.make_async_copy(refs[i], refs[count + i], sem.at[i]) for i in range(count)
    ]
    for copy in copies:
        copy.start()
    for copy in copies:
        copy.wait()


def local(replica_grads, block_owner, left_factor, right_factor, left_root, right_root, moment):
    owners = lax.axis_size("fsdp")
    reps = lax.axis_size("rep")
    rows, width = replica_grads.shape[1:]
    block = left_factor.shape[4]
    cols = width // block
    lane = block // reps
    per_row = block // rows
    half_rows = rows // halves
    sizes = (owners, reps, cols, rows, block, lane, per_row)

    hbm = pl.BlockSpec(memory_space=pltpu.HBM)
    vmem = pl.BlockSpec(memory_space=pltpu.VMEM)
    square = jax.ShapeDtypeStruct((block, block), f32)
    results = (jax.ShapeDtypeStruct((rows, width), bf16), square, square, square)
    others = reps - 1
    by_group = pltpu.SemaphoreType.DMA((halves, 2, others))
    by_half = pltpu.SemaphoreType.DMA((halves,))
    by_side = pltpu.SemaphoreType.DMA((halves, 2, 3))
    by_leg = pltpu.SemaphoreType.DMA((halves, 6))
    flat = [
        array.reshape(block, block)
        for array in (left_root, right_root, left_factor, right_factor, moment)
    ]
    outs = pl.pallas_call(
        functools.partial(kernel, sizes),
        out_shape=results,
        in_specs=[hbm] * 7,
        out_specs=(vmem,) * 4,
        scratch_shapes=[
            pltpu.SMEM(block_owner.shape, jnp.int32),
            pltpu.VMEM((8, 128), jnp.int32),
            pltpu.SMEM((8, 128), jnp.int32),
            pltpu.VMEM((rows, width), bf16),
            pltpu.VMEM((block, block), bf16),
            pltpu.VMEM((block, block), bf16),
            pltpu.VMEM((block, block), f32),
            pltpu.VMEM((block, block), f32),
            pltpu.VMEM((block, block), f32),
            pltpu.VMEM((halves, others, cols, half_rows, lane), bf16),
            pltpu.VMEM((halves, cols + 1, half_rows, lane), bf16),
            pltpu.VMEM((halves, cols, half_rows, lane), bf16),
            [pltpu.VMEM((2, cols + 1, half_rows, lane), bf16)] * halves,
            pltpu.VMEM((halves, owners, half_rows, lane), bf16),
            pltpu.VMEM((block, block), bf16),
            pltpu.VMEM((block, block), f32),
            pltpu.VMEM((reps, halves, per_row, half_rows, lane), bf16),
            pltpu.VMEM((halves, reps, per_row, half_rows, lane), bf16),
            [pltpu.VMEM((owners, half_rows, lane), bf16)] * halves,
            pltpu.VMEM((halves, reps, cols, half_rows, lane), bf16),
            pltpu.SemaphoreType.DMA((7,)),
            pltpu.SemaphoreType.DMA,
            by_side,
            by_side,
            by_half,
            by_half,
            by_group,
            by_group,
            by_half,
            by_half,
            by_leg,
            by_leg,
        ]
        + [pltpu.SemaphoreType.REGULAR] * 3,
        compiler_params=pltpu.CompilerParams(
            collective_id=0, has_side_effects=True, vmem_limit_bytes=24 * 1024 * 1024
        ),
    )(
        *(
            pltpu.with_memory_space_constraint(array, pltpu.HBM)
            for array in (block_owner, replica_grads.reshape(rows, width), *flat)
        )
    )

    direction, left_new, right_new, moment_new = pl.pallas_call(
        finish,
        out_shape=results,
        in_specs=[vmem] * 4,
        out_specs=(hbm,) * 4,
        scratch_shapes=[pltpu.SemaphoreType.DMA((4,))],
        compiler_params=pltpu.CompilerParams(vmem_limit_bytes=1024*1024),
    )(*(pltpu.with_memory_space_constraint(array, pltpu.VMEM) for array in outs))
    state_shape = left_factor.shape
    return (
        direction,
        left_new.reshape(state_shape),
        right_new.reshape(state_shape),
        moment_new.reshape(state_shape),
    )


def solution(mesh):
    state = P("fsdp", "rep", None, None, None)
    return jax.shard_map(
        local,
        mesh=mesh,
        in_specs=(P("rep", "fsdp", None), P(), state, state, state, state, state),
        out_specs=(P("fsdp", None), state, state, state),
        check_vma=False,
    )
```

```python
import functools

import jax
import jax.numpy as jnp
from jax import lax
from jax.experimental import pallas as pl
from jax.experimental.pallas import tpu as pltpu
from jax.sharding import PartitionSpec as P

MESH = pl.DeviceIdType.MESH

stat_decay = 0.9
graft_decay = 0.99
adam_epsilon = 1e-08
graft_epsilon = 1e-06

bf16 = jnp.bfloat16
f32 = jnp.float32

cores, xs = 2, 4
halves = 2
ways = (1, -1)


def remote(src, dst, send_sem, recv_sem, where):
    return pltpu.make_async_remote_copy(
        src_ref=src,
        dst_ref=dst,
        send_sem=send_sem,
        recv_sem=recv_sem,
        device_id=where,
        device_id_type=MESH,
    )


def settle(ref, sem):
    pltpu.make_async_copy(ref, ref, sem).wait()


def greet(sem, to_f, to_y):
    pl.semaphore_signal(sem, inc=1, device_id=(to_f, to_y), device_id_type=MESH)


def kernel(
    sizes,
    owner_hbm,
    grads_hbm,
    left_root_hbm,
    right_root_hbm,
    left_hbm,
    right_hbm,
    moment_hbm,
    direction_ref,
    left_new_ref,
    right_new_ref,
    moment_new_ref,
    owner,
    pick_row,
    pick,
    grads,
    left_root,
    right_root,
    left,
    right,
    moment,
    stage,
    mine,
    via,
    parts,
    outbox,
    g_land,
    conditioned,
    stepped,
    relay,
    arrived,
    chosen,
    load_sem,
    pick_sem,
    part_send,
    part_recv,
    out_send,
    out_recv,
    relay_send,
    relay_recv,
    back_send,
    back_recv,
    choice_send,
    choice_recv,
    *round_sems,
):
    owners, reps, cols, rows, block, lane, per_row = sizes
    half_rows = rows // halves
    f = lax.axis_index("fsdp")
    y = lax.axis_index("rep")
    home = f // per_row
    place = f % per_row
    own_plane = home == y

    def replica(d):
        return (y + d + reps) % reps

    loads = [
        pltpu.make_async_copy(source, target, load_sem.at[number])
        for number, (source, target) in enumerate(
            (
                (grads_hbm, grads),
                (owner_hbm, owner),
                (left_root_hbm, left_root),
                (right_root_hbm, right_root),
                (moment_hbm, moment),
                (left_hbm, left),
                (right_hbm, right),
            )
        )
    ]
    for load in loads[:2]:
        load.start()

    zs = owners // (cores * xs)
    core, x, z = f % cores, f // cores % xs, f // (cores * xs)

    def at(dz, dx, dcore):
        return (((z + dz + zs) % zs) * xs + (x + dx + xs) % xs) * cores + (core + dcore) % cores

    replicas = [(f, replica(d)) for d in range(1, reps)]
    close = [(at(d, 0, 0), y) for d in (1, -1, 2, -2)]
    layer = [(at(0, dx, dcore), y) for dx in range(xs) for dcore in range(cores) if dx or dcore]
    near = replicas + close + layer
    rounds = (close, close[2:], replicas)
    barrier = pltpu.get_barrier_semaphore()
    for where in near:
        greet(barrier, *where)

    def set_out(d):
        for h in range(halves):

            @pl.loop(0, cols, unroll=True)
            def _(c):
                start = pl.multiple_of(c * block + replica(d) * lane, lane)
                piece = grads[h * half_rows : (h + 1) * half_rows, pl.ds(start, lane)]
                if d:
                    stage[h, d - 1, c] = piece
                else:
                    mine[h, c] = piece

    loads[0].wait()
    set_out(2)

    spans = ((0, (cols + 1) // 2), ((cols + 1) // 2, cols))

    def part_copy(h, side, leg):
        way, (first, last) = ways[side], spans[side]
        span = pl.ds(first, last - first)
        source, target, where = (
            (stage.at[h, 1, span], via.at[h, span], replica(way)),
            (stage.at[h, -way % reps - 1, span], parts[h].at[1, span], replica(-way)),
            (stage.at[h, way % reps - 1, span], parts[h].at[0, span], replica(way)),
        )[leg]
        return remote(
            source, target, part_send.at[h, side, leg], part_recv.at[h, side, leg], (f, where)
        )

    def send_parts(h, leg):
        for side in range(2):
            part_copy(h, side, leg).start()

    def pass_on(h):
        for side in range(2):
            part_copy(h, side, 0).wait_recv()
            slot = ways[side] % reps - 1

            @pl.loop(*spans[side], unroll=True)
            def _(c):
                both = stage[h, slot, c].astype(f32) + via[h, c].astype(f32)
                stage[h, slot, c] = both.astype(bf16)

            part_copy(h, side, 2).start()

    pl.semaphore_wait(barrier, len(near))
    send_parts(0, 0)
    send_parts(1, 0)
    set_out(1)
    set_out(3)
    send_parts(0, 1)
    for where in rounds[0]:
        greet(round_sems[0], *where)
    for load in loads[2:]:
        load.start()
    set_out(0)
    for h in range(halves):
        nothing = jnp.zeros((half_rows, lane), bf16)
        mine[h, cols] = nothing
        for d in range(2):
            parts[h][d, cols] = nothing

    loads[1].wait()
    owner_of_lane = lax.broadcasted_iota(jnp.int32, pick_row.shape, 1)
    picked = jnp.full(pick_row.shape, cols, jnp.int32)
    for c in range(cols):
        picked = jnp.where(owner_of_lane == owner[home, c], c, picked)
    pick_row[...] = picked
    pick_copy = pltpu.make_async_copy(pick_row, pick, pick_sem)
    pick_copy.start()
    pick_copy.wait()

    pl.semaphore_wait(round_sems[0], len(rounds[0]))
    for where in rounds[1]:
        greet(round_sems[1], *where)
    pass_on(0)
    send_parts(1, 1)
    pl.semaphore_wait(round_sems[1], len(rounds[1]))
    for where in rounds[2]:
        greet(round_sems[2], *where)
    pass_on(1)
    pl.semaphore_wait(round_sems[2], len(rounds[2]))

    for h in range(halves):
        for leg in (1, 2):
            for side in range(2):
                part_copy(h, side, leg).wait_recv()
        row_start = pl.multiple_of(place * rows + h * half_rows, half_rows)
        target = g_land.at[
            pl.ds(row_start, half_rows), pl.ds(pl.multiple_of(y * lane, lane), lane)
        ]

        @pl.loop(0, owners)
        def _(o):
            col = pick[0, o]
            total = mine[h, col].astype(f32)
            for d in range(2):
                total = total + parts[h][d, col].astype(f32)
            outbox[h, o] = total.astype(bf16)
            here = own_plane & (o == f)

            @pl.when(jnp.logical_not(here))
            def _():
                remote(
                    outbox.at[h, o], target, out_send.at[h], out_recv.at[h], (o, home)
                ).start()

            @pl.when(here)
            def _():
                pltpu.make_async_copy(outbox.at[h, o], target, out_recv.at[h]).start()

    for load in loads[2:]:
        load.wait()
    for h in range(halves):
        settle(arrived[h], out_recv.at[h])

    half = jnp.dot(left_root[...], g_land[...], preferred_element_type=f32).astype(bf16)
    conditioned[...] = jnp.dot(half, right_root[...], preferred_element_type=f32)
    gradient = g_land[...].astype(f32)
    moment_new = graft_decay * moment[...] + (1.0 - graft_decay) * gradient * gradient
    moment_new_ref[...] = moment_new
    adam_step = gradient / (jnp.sqrt(moment_new) + adam_epsilon)
    count = float(block * block)
    adam_mean = jnp.sum(adam_step * adam_step) / count
    cond = conditioned[...]
    cond_mean = jnp.sum(cond * cond) / count
    ratio = (adam_mean + graft_epsilon) / (cond_mean + graft_epsilon)
    scale = jnp.sqrt(jnp.full((1, 1), ratio, f32))
    for q in range(reps):
        quarter = (scale * conditioned[:, q * lane : (q + 1) * lane]).astype(bf16)
        quarter = quarter.reshape(per_row, halves, half_rows, lane)
        for h in range(halves):
            stepped[q, h] = quarter[:, h]

    groups = [(h, j) for h in range(halves) for j in range(2)]
    group_rows = per_row // 2

    def relay_copy(h, j, d):
        span = pl.ds(j * group_rows, group_rows)
        return remote(
            stepped.at[replica(d), h, span],
            relay.at[h, d, span],
            relay_send.at[h, j, d - 1],
            relay_recv.at[h, j, d - 1],
            (f, replica(d)),
        )

    for h, j in groups[:3]:
        for d in (1, 3, 2):
            relay_copy(h, j, d).start()

    def send_back(h, j):
        @pl.loop(0, reps * group_rows)
        def _(k):
            there = k // group_rows * per_row + j * group_rows + k % group_rows
            row = there // per_row
            source = relay.at[h, (y - row + reps) % reps, there % per_row]
            here = there == f
            target = arrived[h].at[f]

            @pl.when(jnp.logical_not(here))
            def _():
                remote(source, target, back_send.at[h], back_recv.at[h], (there, y)).start()

            @pl.when(here)
            def _():
                pltpu.make_async_copy(source, target, back_recv.at[h]).start()

    for h in range(halves):
        relay[h, 0] = stepped[y, h]
    for number, (h, j) in enumerate(groups):
        for d in (1, 3, 2):
            relay_copy(h, j, d).wait_recv()
            if number + 3 < len(groups):
                relay_copy(*groups[number + 3], d).start()
        send_back(h, j)

    def gram(old, contract):
        product = lax.dot_general(
            g_land[...],
            g_land[...],
            (((contract,), (contract,)), ((), ())),
            preferred_element_type=f32,
        )
        return stat_decay * old[...] + (1.0 - stat_decay) * product

    left_new_ref[...] = gram(left, 1)
    right_new_ref[...] = gram(right, 0)

    def choice_copy(h, leg):
        spread = [pl.ds(first, last - first) for first, last in spans]
        source, span, where = (
            (y, spread[0], replica(1)),
            (y, spread[1], replica(-1)),
            (y, spread[1], replica(1)),
            (y, spread[0], replica(-1)),
            (replica(-1), spread[0], replica(1)),
            (replica(1), spread[1], replica(-1)),
        )[leg]
        piece = chosen.at[h, source, span]
        return remote(piece, piece, choice_send.at[h, leg], choice_recv.at[h, leg], (f, where))

    for h in range(halves):
        settle(arrived[h], back_recv.at[h])

        @pl.loop(0, cols, unroll=True)
        def _(c):
            chosen[h, y, c] = arrived[h][owner[home, c]]

        for leg in range(4):
            choice_copy(h, leg).start()

    def place_quarter(h, q):
        @pl.loop(0, cols, unroll=True)
        def _(c):
            start = pl.multiple_of(c * block + q * lane, lane)
            direction_ref[h * half_rows : (h + 1) * half_rows, pl.ds(start, lane)] = chosen[h, q, c]

    for h in range(halves):
        for leg in (0, 1):
            choice_copy(h, leg).wait_recv()
            choice_copy(h, leg + 4).start()
    for h in range(halves):
        place_quarter(h, y)
        for leg in (2, 3):
            choice_copy(h, leg).wait_recv()
        for d in (-1, 1):
            place_quarter(h, replica(d))
    for h in range(halves):
        for leg in (4, 5):
            choice_copy(h, leg).wait_recv()
        place_quarter(h, replica(2))

    for h in range(halves):
        for d in range(1, reps):
            for side in range(2):
                part_copy(h, side, d - 1).wait_send()
            for j in range(2):
                relay_copy(h, j, d).wait_send()
        for leg in range(6):
            choice_copy(h, leg).wait_send()
        settle(outbox.at[h, pl.ds(0, owners - 1)], out_send.at[h])

        @pl.when(jnp.logical_not(own_plane))
        def _():
            settle(outbox.at[h, owners - 1], out_send.at[h])

        settle(arrived[h].at[pl.ds(0, owners - 1)], back_send.at[h])


def finish(*refs):
    count = len(refs) // 2
    sem = refs[-1]
    copies = [
        pltpu.make_async_copy(refs[i], refs[count + i], sem.at[i]) for i in range(count)
    ]
    for copy in copies:
        copy.start()
    for copy in copies:
        copy.wait()


def local(replica_grads, block_owner, left_factor, right_factor, left_root, right_root, moment):
    owners = lax.axis_size("fsdp")
    reps = lax.axis_size("rep")
    rows, width = replica_grads.shape[1:]
    block = left_factor.shape[4]
    cols = width // block
    lane = block // reps
    per_row = block // rows
    half_rows = rows // halves
    sizes = (owners, reps, cols, rows, block, lane, per_row)

    hbm = pl.BlockSpec(memory_space=pltpu.HBM)
    vmem = pl.BlockSpec(memory_space=pltpu.VMEM)
    square = jax.ShapeDtypeStruct((block, block), f32)
    results = (jax.ShapeDtypeStruct((rows, width), bf16), square, square, square)
    others = reps - 1
    by_group = pltpu.SemaphoreType.DMA((halves, 2, others))
    by_half = pltpu.SemaphoreType.DMA((halves,))
    by_side = pltpu.SemaphoreType.DMA((halves, 2, 3))
    by_leg = pltpu.SemaphoreType.DMA((halves, 6))
    flat = [
        array.reshape(block, block)
        for array in (left_root, right_root, left_factor, right_factor, moment)
    ]
    outs = pl.pallas_call(
        functools.partial(kernel, sizes),
        out_shape=results,
        in_specs=[hbm] * 7,
        out_specs=(vmem,) * 4,
        scratch_shapes=[
            pltpu.SMEM(block_owner.shape, jnp.int32),
            pltpu.VMEM((8, 128), jnp.int32),
            pltpu.SMEM((8, 128), jnp.int32),
            pltpu.VMEM((rows, width), bf16),
            pltpu.VMEM((block, block), bf16),
            pltpu.VMEM((block, block), bf16),
            pltpu.VMEM((block, block), f32),
            pltpu.VMEM((block, block), f32),
            pltpu.VMEM((block, block), f32),
            pltpu.VMEM((halves, others, cols, half_rows, lane), bf16),
            pltpu.VMEM((halves, cols + 1, half_rows, lane), bf16),
            pltpu.VMEM((halves, cols, half_rows, lane), bf16),
            [pltpu.VMEM((2, cols + 1, half_rows, lane), bf16)] * halves,
            pltpu.VMEM((halves, owners, half_rows, lane), bf16),
            pltpu.VMEM((block, block), bf16),
            pltpu.VMEM((block, block), f32),
            pltpu.VMEM((reps, halves, per_row, half_rows, lane), bf16),
            pltpu.VMEM((halves, reps, per_row, half_rows, lane), bf16),
            [pltpu.VMEM((owners, half_rows, lane), bf16)] * halves,
            pltpu.VMEM((halves, reps, cols, half_rows, lane), bf16),
            pltpu.SemaphoreType.DMA((7,)),
            pltpu.SemaphoreType.DMA,
            by_side,
            by_side,
            by_half,
            by_half,
            by_group,
            by_group,
            by_half,
            by_half,
            by_leg,
            by_leg,
        ]
        + [pltpu.SemaphoreType.REGULAR] * 3,
        compiler_params=pltpu.CompilerParams(
            collective_id=0, has_side_effects=True, vmem_limit_bytes=24 * 1024 * 1024
        ),
    )(
        *(
            pltpu.with_memory_space_constraint(array, pltpu.HBM)
            for array in (block_owner, replica_grads.reshape(rows, width), *flat)
        )
    )

    direction, left_new, right_new, moment_new = pl.pallas_call(
        finish,
        out_shape=results,
        in_specs=[vmem] * 4,
        out_specs=(hbm,) * 4,
        scratch_shapes=[pltpu.SemaphoreType.DMA((4,))],
        compiler_params=pltpu.CompilerParams(vmem_limit_bytes=1024*1024),
    )(*(pltpu.with_memory_space_constraint(array, pltpu.VMEM) for array in outs))
    state_shape = left_factor.shape
    return (
        direction,
        left_new.reshape(state_shape),
        right_new.reshape(state_shape),
        moment_new.reshape(state_shape),
    )


def solution(mesh):
    state = P("fsdp", "rep", None, None, None)
    return jax.shard_map(
        local,
        mesh=mesh,
        in_specs=(P("rep", "fsdp", None), P(), state, state, state, state, state),
        out_specs=(P("fsdp", None), state, state, state),
        check_vma=False,
    )
```
